32 devices in a mesh: groups: 2 (over y), row: 4 (over z), col: 2 (over x), sub: 2 (over core).
Axes of the slice: x: 2, y: 2, z: 4, core: 2. Of those that a mesh axis runs over, the one named last changes fastest.
Arguments:
- densities: float32 [2, 4, 32768], P(None, None, ('groups', 'row', 'col', 'sub')), parts along dimension 2, may hold values from -6 to 6
- positions: float32 [3, 32768], P(None, ('groups', 'row', 'col', 'sub')), parts along dimension 1, may hold values from -5 to 5
- normals: float32 [3, 32768], P(None, ('groups', 'row', 'col', 'sub')), parts along dimension 1, may hold values from -3 to 3
- weights: float32 [32768], P(('groups', 'row', 'col', 'sub')), parts along dimension 0, may hold values from 0.3 to 1
- cluster_panels: int32 [32, 1024], P(('groups', 'row', 'col', 'sub')), parts along dimension 0, may hold values from 0 to 1023, each once within a row
- pair_list: int32 [2, 384], P(None, ('groups', 'row', 'col', 'sub')), parts along dimension 1, may hold values from 0 to 31, as said below
- quad_order: int32 [384], P(('groups', 'row', 'col', 'sub')), parts along dimension 0, may hold values from 1 to 4
- pair_count: int32 [32], P(('groups', 'row', 'col', 'sub')), parts along dimension 0, may hold values from 3 to 12, as said below
Outputs:
- layer_potentials: float32 [2, 4, 32768], P(None, None, ('groups', 'row', 'col', 'sub')), parts along dimension 2
The draws below stay inside these ranges and needn't reach their ends.
There are 2 independent parts, one for each index of `groups`. The reference program is written for one: setup_inputs(seed, part) draws one part's arguments, and reference() takes and returns one part's arrays. A program takes and returns all parts, laid end to end along the dimension named above; each array names one. Nothing has to cross between parts.
Inputs may be any that keep to these rules, and one draw needn't show every extreme that they name: `pair_list`: row 0 lies below 16 and row 1 below 32; every slot, used or not, holds a valid pair; no unordered pair of clusters stands in two slots of a problem, and a cluster may be paired with itself. `pair_count`: the used slots of a device are its first ones; the two devices of one grid cell hold 15 used slots together, and some device holds exactly 12.
All inputs are finite; a program needn't handle non-finite values.
Results may differ from the reference program's by a relative error of at most 0.0003.
Values sent between devices are 32-bit elements; how exact they have to be, the bound alone decides.
A program may use at most 128 MiB of HBM per device.

```python
import math
import jax
import jax.numpy as jnp
from jax import lax

PANEL = 256
NRHS = 4
CL_DEV = 4
CAP = 12
ROWS_GRID = 4
COLS_GRID = 2
SUBS = 2
TILES = 16
PAN_DEV = 1024
PANELS = 16384
ROW_CL = 16
COL_CL = 32


def draw_pair_count(key, part):
    key = jax.random.fold_in(key, 5)
    count_key, pick_key = jax.random.split(key)
    chips = TILES // SUBS
    first = jax.random.randint(count_key, (chips,), CAP // 4, CAP + 1)
    chosen = jax.random.randint(pick_key, (), 0, chips)
    first = jnp.where(jnp.arange(chips) == chosen, CAP, first)
    second = CAP + CAP // 4 - first
    return jnp.stack([first, second], axis=1).reshape(TILES).astype(jnp.int32)


def draw_pair_list(key, part):
    key = jax.random.fold_in(key, 7)
    combos = ROW_CL * COL_CL
    combo_ids = jnp.arange(combos, dtype=jnp.int32)
    row_local = combo_ids // COL_CL
    col_local = combo_ids % COL_CL
    chips = ROWS_GRID * COLS_GRID

    def one_chip(chip_key, chip_id):
        row_of = chip_id // COLS_GRID
        col_of = chip_id % COLS_GRID
        first_cl = row_of * ROW_CL + row_local
        second_cl = ((col_local // (SUBS * CL_DEV) * COLS_GRID + col_of) * SUBS + col_local // CL_DEV % SUBS) * CL_DEV + col_local % CL_DEV
        is_kept = (first_cl == second_cl) | ((first_cl < second_cl) == ((first_cl + second_cl) % 2 == 0))
        noise = jax.random.randint(chip_key, (combos,), 0, 2048)
        score = jnp.where(is_kept, noise, 2048) * combos + combo_ids
        _, picked = lax.top_k(-score, SUBS * CAP)
        return picked
    picked = jax.vmap(one_chip)(jax.random.split(key, chips), jnp.arange(chips, dtype=jnp.int32))
    picked = picked.reshape(TILES * CAP)
    return jnp.stack([picked // COL_CL, picked % COL_CL]).astype(jnp.int32)


def set_ends(values, key, low, largest):
    shape = values.shape
    spot = [jax.random.randint(jax.random.fold_in(key, axis), (), 0, shape[axis]) for axis in range(len(shape))]
    values = values.at[tuple(spot)].set(low)
    longest = shape.index(max(shape))
    spot[longest] = (spot[longest] + 1) % shape[longest]
    return values.at[tuple(spot)].set(largest)


def shard_levels(own_key, extent, pieces, low, top_value):
    loudness = 1.0
    for axis_at, shards_of in pieces:
        draws = jax.random.uniform(jax.random.fold_in(jax.random.fold_in(own_key, 6), axis_at), (shards_of,), jnp.float32, low / len(pieces), top_value / len(pieces))
        loudness = loudness * jnp.repeat(jnp.exp(draws), extent[axis_at] // shards_of).reshape((-1,) + (1,) * (len(extent) - 1 - axis_at))
    return loudness


def normal_values(key, extent, scale, reach, cuts=(), held_as=jnp.bfloat16):
    result = jax.random.normal(key, extent, jnp.float32) * scale
    if len(cuts) > 0:
        result = shard_levels(key, extent, cuts, -0.22, 0.18) * result
    return jnp.clip(result, min=-reach, max=reach).astype(held_as)


def setup_inputs(seed: int = 0, part: int = 0) -> dict:
    key_list = jax.random.split(jax.random.key(seed), 9)
    part_splits = jax.random.split(jax.random.fold_in(key_list[8], part), 9)
    return {
        "densities": normal_values(part_splits[0], (2, NRHS, PANELS), 1.0, 6.0, ((2, 16),), jnp.float32),
        "positions": normal_values(part_splits[1], (3, PANELS), 1.0, 5.0, ((1, 16),), jnp.float32),
        "normals": normal_values(part_splits[2], (3, PANELS), 0.5, 3.0, ((1, 16),), jnp.float32),
        "weights": jnp.clip(jnp.exp(math.log(1.0) - 1.2039728 * jax.random.uniform(part_splits[3], (PANELS,), jnp.float32) ** shard_levels(part_splits[3], (PANELS,), ((0, 16),), -0.2, 0.2)), 0.3, 1.0),
        "cluster_panels": jax.vmap(lambda own: jax.random.permutation(own, PAN_DEV))(jax.random.split(part_splits[4], TILES)).reshape((TILES, PAN_DEV)).astype(jnp.int32),
        "pair_list": draw_pair_list(jax.random.fold_in(jax.random.fold_in(key_list[8], part), 71), part),
        "quad_order": set_ends(jax.random.randint(part_splits[6], (TILES * CAP,), 1, 5), jax.random.fold_in(part_splits[6], 1), 1, 4).astype(jnp.int32),
        "pair_count": draw_pair_count(jax.random.fold_in(jax.random.fold_in(key_list[8], part), 71), part),
    }


wavenumber = 3.0
soften = 0.5
four_pi = 12.566370614359172

def kernels(row_geom, col_geom, quad_level):
    offset = row_geom[0:3, :, None] - col_geom[0:3, None, :]
    soften_sq = (soften / quad_level.astype(jnp.float32)) ** 2
    rho_sq = lax.optimization_barrier(jnp.sum(offset * offset, axis=0)) + soften_sq
    distance = jnp.sqrt(rho_sq)
    phase_arg = wavenumber * distance
    cosine = jnp.cos(phase_arg)
    single = cosine / (four_pi * distance)
    radial = (cosine + phase_arg * jnp.sin(phase_arg)) / (four_pi * rho_sq * distance)
    row_weight = row_geom[6][:, None]
    col_weight = col_geom[6][None, :]
    along_col = lax.optimization_barrier(jnp.sum(offset * col_geom[3:6, None, :], axis=0))
    along_row = lax.optimization_barrier(jnp.sum(offset * row_geom[3:6, :, None], axis=0))
    return (row_weight * col_weight * single, row_weight * radial * along_col, -col_weight * radial * along_row)

def apply_rows(tile, dens):
    return jnp.einsum('ij,rj->ri', tile, dens, precision=lax.Precision.HIGHEST)

def apply_cols(tile, dens):
    return jnp.einsum('ij,ri->rj', tile, dens, precision=lax.Precision.HIGHEST)

def contributions(row_geom, col_geom, quad_level, nrhs):
    single, double, adjoint = kernels(row_geom, col_geom, quad_level)
    row_sigma = row_geom[7:7 + nrhs]
    row_mu = row_geom[7 + nrhs:]
    col_sigma = col_geom[7:7 + nrhs]
    col_mu = col_geom[7 + nrhs:]
    onto_row = jnp.stack([apply_rows(single, col_sigma) + apply_rows(double, col_mu), apply_rows(adjoint, col_sigma)])
    onto_col = jnp.stack([apply_cols(single, row_sigma) + apply_cols(adjoint, row_mu), apply_cols(double, row_sigma)])
    return (onto_row, onto_col)

def reference(densities, positions, normals, weights, cluster_panels, pair_list, quad_order, pair_count):
    stacked = jnp.concatenate([positions, normals, weights[None, :], densities.reshape(2 * NRHS, PANELS)], axis=0)
    source = jnp.arange(PANELS, dtype=jnp.int32) // PAN_DEV * PAN_DEV + cluster_panels.reshape(PANELS).astype(jnp.int32)
    ordered = stacked[:, source]
    slot_ids = jnp.arange(TILES * CAP, dtype=jnp.int32)
    device_ids = slot_ids // CAP
    row_of = device_ids // (COLS_GRID * SUBS)
    col_of = device_ids // SUBS % COLS_GRID
    row_cluster = row_of * ROW_CL + pair_list[0]
    local_col = pair_list[1]
    col_cluster = ((local_col // (SUBS * CL_DEV) * COLS_GRID + col_of) * SUBS + local_col // CL_DEV % SUBS) * CL_DEV + local_col % CL_DEV
    is_live = slot_ids % CAP < pair_count[device_ids]

    def slot_step(potentials, slot_item):
        first_cl, second_cl, quad_level, in_use = slot_item
        row_geom = lax.dynamic_slice_in_dim(ordered, (first_cl * PANEL).astype(jnp.int32), PANEL, 1)
        col_geom = lax.dynamic_slice_in_dim(ordered, (second_cl * PANEL).astype(jnp.int32), PANEL, 1)
        onto_row, onto_col = contributions(row_geom, col_geom, quad_level, NRHS)
        onto_row = jnp.where(in_use, onto_row, 0.0)
        onto_col = jnp.where(in_use & (first_cl != second_cl), onto_col, 0.0)
        row_start = (first_cl * PANEL).astype(jnp.int32)
        current = lax.dynamic_slice_in_dim(potentials, row_start, PANEL, 2)
        potentials = lax.dynamic_update_slice_in_dim(potentials, current + onto_row, row_start, 2)
        col_start = (second_cl * PANEL).astype(jnp.int32)
        current = lax.dynamic_slice_in_dim(potentials, col_start, PANEL, 2)
        potentials = lax.dynamic_update_slice_in_dim(potentials, current + onto_col, col_start, 2)
        return (potentials, None)
    potentials = jnp.zeros((2, NRHS, PANELS), jnp.float32)
    potentials, _ = lax.scan(slot_step, potentials, (row_cluster, col_cluster, quad_order, is_live))
    return jnp.zeros((2, NRHS, PANELS), jnp.float32).at[:, :, source].set(potentials)
```

```python
import functools
import math

import jax
import jax.numpy as jnp
import numpy as np
from jax import lax
from jax.experimental import pallas as pl
from jax.experimental.pallas import tpu as pltpu
from jax.sharding import PartitionSpec as P

MESH = pl.DeviceIdType.MESH
PANEL = 256
HALF = 128
WAVENUMBER = 3.0
SOFTEN = 0.5
FOUR_PI = 4.0 * math.pi
F32 = jnp.float32
BF16 = jnp.bfloat16
CHUNK = 16


def fit(func, degree):
    cheb = np.polynomial.chebyshev.Chebyshev.interpolate(func, degree, domain=[0.0, 0.2501])
    return [float(v) for v in cheb.convert(kind=np.polynomial.Polynomial).coef]


def sinc_turn(z):
    f = np.sqrt(np.maximum(z, 1e-30))
    return np.sin(2 * np.pi * f) / f


COS_COEF = [v / FOUR_PI for v in fit(lambda z: np.cos(2 * np.pi * np.sqrt(np.maximum(z, 0.0))), 6)]
SIN_COEF = [v * WAVENUMBER / FOUR_PI for v in fit(sinc_turn, 6)]


def horner(coef, z):
    value = coef[-1] * z + coef[-2]
    for c in coef[-3::-1]:
        value = value * z + c
    return value


def two_parts(value):
    hi = value.astype(BF16)
    lo = (value - hi.astype(F32)).astype(BF16)
    return hi, lo


def three_parts(value):
    hi = value.astype(BF16).astype(F32)
    rest = value - hi
    mid = rest.astype(BF16).astype(F32)
    return jnp.concatenate([hi, mid, rest - mid], axis=0)


def tile_parts(e, n_i, n_j, soften_sq):
    rho_sq = e[0] * e[0] + e[1] * e[1] + e[2] * e[2] + soften_sq
    inv = lax.rsqrt(rho_sq)
    rho = rho_sq * inv
    turns = rho * (WAVENUMBER / (2 * math.pi))
    f = turns - jnp.round(turns)
    z = f * f
    cosine = horner(COS_COEF, z)
    radial = (cosine + rho * f * horner(SIN_COEF, z)) * (inv * inv * inv)
    double = radial * (e[0] * n_j[0] + e[1] * n_j[1] + e[2] * n_j[2])
    adjoint = radial * (e[0] * n_i[0] + e[1] * n_i[1] + e[2] * n_i[2])
    return cosine * inv, double, adjoint


def kernel(
    sizes,
    dens_ref, pos_ref, nrm_ref, wgt_ref, order_ref, pair_ref, quad_ref, count_ref,
    out_ref,
    onehot, stacked, meta, meta_s, row_buf, col_half, col_buf,
    tiles, row_term, col_term, row_send, col_send, row_recv, col_recv,
    meta_sem, local_sem, row_ssem, row_rsem, col_ssem, col_rsem,
    row_ssem2, row_rsem2, col_ssem2, col_rsem2,
):
    n_row, n_col, n_sub, cl_dev, slots, used = sizes
    own = cl_dev * PANEL
    row_devs = n_col * n_sub
    col_devs = n_row * n_sub
    r = lax.axis_index("row")
    c = lax.axis_index("col")
    s = lax.axis_index("sub")
    me_row = c * n_sub + s
    me_col = r * n_sub + s

    def row_peer(d):
        idx = lax.rem(me_row + d, row_devs)
        return idx, {"col": idx // n_sub, "sub": lax.rem(idx, n_sub)}

    def col_peer(d):
        idx = lax.rem(me_col + d, col_devs)
        return idx, {"row": idx // n_sub, "sub": lax.rem(idx, n_sub)}

    barrier = pltpu.get_barrier_semaphore()
    for d in range(1, row_devs):
        pl.semaphore_signal(barrier, inc=1, device_id=row_peer(d)[1], device_id_type=MESH)
    for d in range(1, col_devs):
        pl.semaphore_signal(barrier, inc=1, device_id=col_peer(d)[1], device_id_type=MESH)

    def fill(t, carry):
        base = pl.multiple_of(t * 64, 64)
        ids = lax.broadcasted_iota(jnp.int32, (64, own), 0) + base
        onehot[pl.ds(base, 64), :] = jnp.where(ids == order_ref[...], 1.0, 0.0).astype(BF16)
        return carry

    lax.fori_loop(0, own // 64, fill, 0)

    stacked[0:3, :] = pos_ref[...]
    stacked[3:6, :] = nrm_ref[...]
    stacked[6:8, :] = jnp.zeros((2, own), F32)
    stacked[8:12, :] = dens_ref[0] * wgt_ref[...]
    stacked[12:16, :] = dens_ref[1]
    meta[0] = jnp.zeros((8, 128), jnp.int32)
    meta[0, 0:2, 0:slots] = pair_ref[...]
    meta[0, 2:3, 0:slots] = quad_ref[...]
    meta[0, 3:4, 0:1] = count_ref[...]
    parts = three_parts(stacked[...]).astype(BF16)
    for g in range(cl_dev):
        got = jnp.dot(parts, onehot[:, g * PANEL : (g + 1) * PANEL], preferred_element_type=F32)
        panels = (got[0:16] + got[16:32]) + got[32:48]
        row_buf[me_row * cl_dev + g] = panels
        for h in range(2):
            col_half[h, g] = panels[:, h * HALF : (h + 1) * HALF]
    col_buf[pl.ds(me_col * cl_dev, cl_dev)] = col_half[s]

    pl.semaphore_wait(barrier, row_devs + col_devs - 2)

    other = 1 - s
    meta_copy = pltpu.make_async_remote_copy(
        src_ref=meta.at[0], dst_ref=meta.at[1], send_sem=meta_sem.at[0], recv_sem=meta_sem.at[1],
        device_id={"sub": other}, device_id_type=MESH,
    )
    meta_copy.start()

    def col_copy(d):
        idx, dev = col_peer(d)
        there = pl.ds(me_col * cl_dev, cl_dev)
        return pltpu.make_async_remote_copy(
            src_ref=col_half.at[dev["sub"]], dst_ref=col_buf.at[there],
            send_sem=col_ssem.at[d], recv_sem=col_rsem.at[d],
            device_id=dev, device_id_type=MESH,
        )

    def row_copy(d):
        idx, dev = row_peer(d)
        here = pl.ds(me_row * cl_dev, cl_dev)
        return pltpu.make_async_remote_copy(
            src_ref=row_buf.at[here], dst_ref=row_buf.at[here],
            send_sem=row_ssem.at[d], recv_sem=row_rsem.at[d],
            device_id=dev, device_id_type=MESH,
        )

    def col_arrived(d):
        idx = lax.rem(me_col + col_devs - d, col_devs)
        here = pl.ds(idx * cl_dev, cl_dev)
        pltpu.make_async_remote_copy(
            src_ref=col_half.at[0], dst_ref=col_buf.at[here],
            send_sem=col_ssem.at[d], recv_sem=col_rsem.at[d],
            device_id={"sub": other}, device_id_type=MESH,
        ).wait_recv()

    def row_arrived(d):
        idx = lax.rem(me_row + row_devs - d, row_devs)
        here = pl.ds(idx * cl_dev, cl_dev)
        pltpu.make_async_remote_copy(
            src_ref=row_buf.at[here], dst_ref=row_buf.at[here],
            send_sem=row_ssem.at[d], recv_sem=row_rsem.at[d],
            device_id={"sub": other}, device_id_type=MESH,
        ).wait_recv()

    for d in range(1, col_devs):
        col_copy(d).start()
    for d in range(1, row_devs):
        row_copy(d).start()

    meta_copy.wait()
    to_smem = pltpu.make_async_copy(meta, meta_s, local_sem)
    to_smem.start()
    to_smem.wait()
    for d in range(1, row_devs):
        row_arrived(d)
    for d in range(1, col_devs):
        col_arrived(d)

    first_rows = lax.broadcasted_iota(jnp.int32, (8, HALF), 0) < 4
    first_rows_wide = lax.broadcasted_iota(jnp.int32, (8, PANEL), 0) < 4

    def slot_of(k):
        count0 = jnp.where(s == 0, meta_s[0, 3, 0], meta_s[1, 3, 0])
        is_first = k < count0
        bank = jnp.where(is_first, s, 1 - s)
        at = jnp.where(is_first, k, k - count0)
        return meta_s[bank, 0, at], meta_s[bank, 1, at], meta_s[bank, 2, at]

    def swap(v):
        return jnp.concatenate([v[4:8], v[0:4]], axis=0)

    def one_slot(k, carry):
        v, u, q = slot_of(k)
        x_i = row_buf[v]
        y_j = col_buf[u]
        q_f = jnp.full((1, PANEL), q, jnp.int32).astype(F32)
        soften_sq = (SOFTEN / q_f) * (SOFTEN / q_f)
        t_j = jnp.transpose(y_j[0:8])
        for m in range(HALF // CHUNK):
            at = slice(m * CHUNK, (m + 1) * CHUNK)
            e = [x_i[a : a + 1] - t_j[at, a : a + 1] for a in range(3)]
            n_i = [x_i[3 + a : 4 + a] for a in range(3)]
            n_j = [t_j[at, 3 + a : 4 + a] for a in range(3)]
            for b, value in enumerate(tile_parts(e, n_i, n_j, soften_sq)):
                hi, lo = two_parts(value)
                tiles[b * 2 * HALF + m * CHUNK : b * 2 * HALF + (m + 1) * CHUNK, :] = hi
                tiles[b * 2 * HALF + HALF + m * CHUNK : b * 2 * HALF + HALF + (m + 1) * CHUNK, :] = lo
        d_j = y_j[8:16]
        s_j = swap(d_j)
        sig = jnp.where(first_rows, d_j, 0.0)
        mu = jnp.where(first_rows, s_j, 0.0)
        adj = jnp.where(first_rows, 0.0, -s_j)

        def stack_parts(value):
            hi = value.astype(BF16).astype(F32)
            return jnp.concatenate([hi, value - hi], axis=0).astype(BF16)

        sig, mu, adj = stack_parts(sig), stack_parts(mu), stack_parts(adj)
        lhs = jnp.concatenate([sig, sig, mu, mu, adj, adj], axis=1)
        got = jnp.dot(lhs, tiles[...], preferred_element_type=F32)
        row_term[k] = got[0:8] + got[8:16]
        lhs = stack_parts(x_i[8:16])
        got = lax.dot_general(lhs, tiles[...], (((1,), (1,)), ((), ())), preferred_element_type=F32)
        got = got[0:8] + got[8:16]
        t = [got[:, b * 2 * HALF : b * 2 * HALF + HALF] + got[:, b * 2 * HALF + HALF : (b + 1) * 2 * HALF] for b in range(3)]
        col_term[k] = jnp.where(first_rows, t[0] - swap(t[2]), swap(t[1]))
        return carry

    lax.fori_loop(0, used, one_slot, 0)

    slot_info = [slot_of(k) for k in range(used)]
    row_ids = [info[0] for info in slot_info]
    col_ids = []
    for v, u, _ in slot_info:
        a = r * (cl_dev * row_devs) + v
        per = n_sub * cl_dev
        b = ((u // per * n_col + c) * n_sub + lax.rem(u // cl_dev, n_sub)) * cl_dev + lax.rem(u, cl_dev)
        col_ids.append(jnp.where(a == b, -1, u))

    def col_sum(idx, g):
        total = jnp.zeros((8, HALF), F32)
        for k in range(used):
            total += jnp.where(col_ids[k] == idx * cl_dev + g, col_term[k], 0.0)
        return total

    def row_sum(idx, g):
        total = jnp.zeros((8, PANEL), F32)
        for k in range(used):
            total += jnp.where(row_ids[k] == idx * cl_dev + g, row_term[k], 0.0)
        return total

    def col_back(d):
        idx, dev = col_peer(d)
        return pltpu.make_async_remote_copy(
            src_ref=col_send.at[d], dst_ref=col_recv.at[me_col],
            send_sem=col_ssem2.at[d], recv_sem=col_rsem2.at[d],
            device_id=dev, device_id_type=MESH,
        )

    def row_back(d):
        idx, dev = row_peer(d)
        return pltpu.make_async_remote_copy(
            src_ref=row_send.at[d], dst_ref=row_recv.at[me_row],
            send_sem=row_ssem2.at[d], recv_sem=row_rsem2.at[d],
            device_id=dev, device_id_type=MESH,
        )

    def send_col(d, carry):
        for g in range(cl_dev):
            col_send[d, g] = col_sum(col_peer(d)[0], g)
        col_back(d).start()
        return carry

    def send_row(d, carry):
        for g in range(cl_dev):
            row_send[d, g] = row_sum(row_peer(d)[0], g)
        row_back(d).start()
        return carry

    lax.fori_loop(1, col_devs, send_col, 0)
    lax.fori_loop(1, row_devs, send_row, 0)
    for g in range(cl_dev):
        col_recv[me_col, g] = col_sum(me_col, g)
        row_recv[me_row, g] = row_sum(me_row, g)

    for d in range(1, row_devs):
        row_copy(d).wait_send()
    for d in range(1, col_devs):
        col_copy(d).wait_send()
    for d in range(1, row_devs):
        idx = lax.rem(me_row + row_devs - d, row_devs)
        pltpu.make_async_remote_copy(
            src_ref=row_send.at[d], dst_ref=row_recv.at[idx],
            send_sem=row_ssem2.at[d], recv_sem=row_rsem2.at[d],
            device_id={"sub": other}, device_id_type=MESH,
        ).wait_recv()
    for d in range(1, col_devs):
        idx = lax.rem(me_col + col_devs - d, col_devs)
        pltpu.make_async_remote_copy(
            src_ref=col_send.at[d], dst_ref=col_recv.at[idx],
            send_sem=col_ssem2.at[d], recv_sem=col_rsem2.at[d],
            device_id={"sub": other}, device_id_type=MESH,
        ).wait_recv()

    pieces = []
    for g in range(cl_dev):
        for h in range(2):
            total = row_recv[0, g, :, h * HALF : (h + 1) * HALF]
            for idx in range(1, row_devs):
                total += row_recv[idx, g, :, h * HALF : (h + 1) * HALF]
            for rr in range(n_row):
                total += col_recv[rr * n_sub + h, g]
            pieces.append(total)
    combined = jnp.concatenate(pieces, axis=1)
    parts = jnp.concatenate([three_parts(combined), jnp.zeros((8, own), F32)], axis=0).astype(BF16)
    for g in range(cl_dev):
        at = slice(g * PANEL, (g + 1) * PANEL)
        got = lax.dot_general(parts, onehot[at, :], (((1,), (1,)), ((), ())), preferred_element_type=F32)
        got = (got[0:8] + got[8:16]) + got[16:24]
        out_ref[0, :, at] = got[0:4] * wgt_ref[:, at]
        out_ref[1, :, at] = got[4:8]

    for d in range(1, row_devs):
        row_back(d).wait_send()
    for d in range(1, col_devs):
        col_back(d).wait_send()


def body(densities, positions, normals, weights, cluster_panels, pair_list, quad_order, pair_count):
    n_row, n_col, n_sub = (lax.axis_size(a) for a in ("row", "col", "sub"))
    own = positions.shape[1]
    cl_dev = own // PANEL
    slots = pair_list.shape[1]
    used = slots + slots // 4
    row_devs = n_col * n_sub
    col_devs = n_row * n_sub
    sizes = (n_row, n_col, n_sub, cl_dev, slots, used)
    dma = pltpu.SemaphoreType.DMA
    vmem = pltpu.VMEM
    return pl.pallas_call(
        functools.partial(kernel, sizes),
        out_shape=jax.ShapeDtypeStruct(densities.shape, F32),
        in_specs=[pl.BlockSpec(memory_space=pltpu.VMEM)] * 8,
        out_specs=pl.BlockSpec(memory_space=pltpu.VMEM),
        scratch_shapes=[
            vmem((own, own), BF16),
            vmem((16, own), F32),
            vmem((2, 8, 128), jnp.int32),
            pltpu.SMEM((2, 8, 128), jnp.int32),
            vmem((row_devs * cl_dev, 16, PANEL), F32),
            vmem((2, cl_dev, 16, HALF), F32),
            vmem((col_devs * cl_dev, 16, HALF), F32),
            vmem((6 * HALF, PANEL), BF16),
            vmem((used, 8, PANEL), F32),
            vmem((used, 8, HALF), F32),
            vmem((row_devs, cl_dev, 8, PANEL), F32),
            vmem((col_devs, cl_dev, 8, HALF), F32),
            vmem((row_devs, cl_dev, 8, PANEL), F32),
            vmem((col_devs, cl_dev, 8, HALF), F32),
            dma((2,)),
            dma,
            dma((row_devs,)), dma((row_devs,)), dma((col_devs,)), dma((col_devs,)),
            dma((row_devs,)), dma((row_devs,)), dma((col_devs,)), dma((col_devs,)),
        ],
        compiler_params=pltpu.CompilerParams(
            collective_id=0, has_side_effects=True, vmem_limit_bytes=40 * 1024 * 1024
        ),
    )(
        densities, positions, normals, weights.reshape(1, own), cluster_panels,
        pair_list, quad_order.reshape(1, slots), pair_count.reshape(1, 1),
    )


def solution(mesh):
    split = ("groups", "row", "col", "sub")
    placed = (
        P(None, None, split), P(None, split), P(None, split), P(split),
        P(split, None), P(None, split), P(split), P(split),
    )
    return jax.shard_map(
        body, mesh=mesh, in_specs=placed, out_specs=P(None, None, split), check_vma=False
    )
```

```python
import functools
import math

import jax
import jax.numpy as jnp
import numpy as np
from jax import lax
from jax.experimental import pallas as pl
from jax.experimental.pallas import tpu as pltpu
from jax.sharding import PartitionSpec as P

MESH = pl.DeviceIdType.MESH
PANEL = 256
HALF = 128
WAVENUMBER = 3.0
SOFTEN = 0.5
FOUR_PI = 4.0 * math.pi
F32 = jnp.float32
BF16 = jnp.bfloat16
CHUNK = 16


def fit(func, degree):
    cheb = np.polynomial.chebyshev.Chebyshev.interpolate(func, degree, domain=[0.0, 0.2501])
    return [float(v) for v in cheb.convert(kind=np.polynomial.Polynomial).coef]


def sinc_turn(z):
    f = np.sqrt(np.maximum(z, 1e-30))
    return np.sin(2 * np.pi * f) / f


COS_COEF = [v / FOUR_PI for v in fit(lambda z: np.cos(2 * np.pi * np.sqrt(np.maximum(z, 0.0))), 6)]
SIN_COEF = [v * WAVENUMBER / FOUR_PI for v in fit(sinc_turn, 6)]


def horner(coef, z):
    value = coef[-1] * z + coef[-2]
    for c in coef[-3::-1]:
        value = value * z + c
    return value


def two_parts(value):
    hi = value.astype(BF16)
    lo = (value - hi.astype(F32)).astype(BF16)
    return hi, lo


def three_parts(value):
    hi = value.astype(BF16).astype(F32)
    rest = value - hi
    mid = rest.astype(BF16).astype(F32)
    return jnp.concatenate([hi, mid, rest - mid], axis=0)


def tile_parts(e, n_i, n_j, soften_sq):
    rho_sq = e[0] * e[0] + e[1] * e[1] + e[2] * e[2] + soften_sq
    inv = lax.rsqrt(rho_sq)
    rho = rho_sq * inv
    turns = rho * (WAVENUMBER / (2 * math.pi))
    f = turns - jnp.round(turns)
    z = f * f
    cosine = horner(COS_COEF, z)
    radial = (cosine + rho * f * horner(SIN_COEF, z)) * (inv * inv * inv)
    double = radial * (e[0] * n_j[0] + e[1] * n_j[1] + e[2] * n_j[2])
    adjoint = radial * (e[0] * n_i[0] + e[1] * n_i[1] + e[2] * n_i[2])
    return cosine * inv, double, adjoint


def kernel(
    sizes,
    dens_in, pos_in, nrm_in, wgt_in, order_in, pair_in, quad_in, count_in,
    out_ref,
    dens_ref, pos_ref, nrm_ref, wgt_ref, order_ref, pair_ref, quad_ref, count_ref, in_sem,
    onehot, stacked, meta, meta_s, row_buf, col_half, col_buf,
    tiles, row_term, col_term, row_send, col_send, row_recv, col_recv,
    meta_sem, local_sem, row_ssem, row_rsem, col_ssem, col_rsem,
    row_ssem2, row_rsem2, col_ssem2, col_rsem2,
):
    n_row, n_col, n_sub, cl_dev, slots, used = sizes
    own = cl_dev * PANEL
    row_devs = n_col * n_sub
    col_devs = n_row * n_sub
    r = lax.axis_index("row")
    c = lax.axis_index("col")
    s = lax.axis_index("sub")
    me_row = c * n_sub + s
    me_col = r * n_sub + s

    def row_peer(d):
        idx = lax.rem(me_row + d, row_devs)
        return idx, {"col": idx // n_sub, "sub": lax.rem(idx, n_sub)}

    def col_peer(d):
        idx = lax.rem(me_col + d, col_devs)
        return idx, {"row": idx // n_sub, "sub": lax.rem(idx, n_sub)}

    loads = [
        pltpu.make_async_copy(src, dst, in_sem.at[n])
        for n, (src, dst) in enumerate((
            (order_in, order_ref), (wgt_in, wgt_ref), (dens_in, dens_ref), (pos_in, pos_ref),
            (nrm_in, nrm_ref), (pair_in, pair_ref), (quad_in, quad_ref), (count_in, count_ref),
        ))
    ]
    for load in loads:
        load.start()
    barrier = pltpu.get_barrier_semaphore()
    for d in range(1, row_devs):
        pl.semaphore_signal(barrier, inc=1, device_id=row_peer(d)[1], device_id_type=MESH)
    for d in range(1, col_devs):
        pl.semaphore_signal(barrier, inc=1, device_id=col_peer(d)[1], device_id_type=MESH)

    loads[0].wait()
    def fill(t, carry):
        base = pl.multiple_of(t * 64, 64)
        ids = lax.broadcasted_iota(jnp.int32, (64, own), 0) + base
        onehot[pl.ds(base, 64), :] = jnp.where(ids == order_ref[...], 1.0, 0.0).astype(BF16)
        return carry

    lax.fori_loop(0, own // 64, fill, 0)

    for load in loads[1:]:
        load.wait()
    stacked[0:3, :] = pos_ref[...]
    stacked[3:6, :] = nrm_ref[...]
    stacked[6:8, :] = jnp.zeros((2, own), F32)
    stacked[8:12, :] = dens_ref[0] * wgt_ref[...]
    stacked[12:16, :] = dens_ref[1]
    meta[0] = jnp.zeros((8, 128), jnp.int32)
    meta[0, 0:2, 0:slots] = pair_ref[...]
    meta[0, 2:3, 0:slots] = quad_ref[...]
    meta[0, 3:4, 0:1] = count_ref[...]
    parts = three_parts(stacked[...]).astype(BF16)
    for g in range(cl_dev):
        got = jnp.dot(parts, onehot[:, g * PANEL : (g + 1) * PANEL], preferred_element_type=F32)
        panels = (got[0:16] + got[16:32]) + got[32:48]
        row_buf[me_row * cl_dev + g] = panels
        for h in range(2):
            col_half[h, g] = panels[:, h * HALF : (h + 1) * HALF]
    col_buf[pl.ds(me_col * cl_dev, cl_dev)] = col_half[s]

    pl.semaphore_wait(barrier, row_devs + col_devs - 2)

    other = 1 - s
    meta_copy = pltpu.make_async_remote_copy(
        src_ref=meta.at[0], dst_ref=meta.at[1], send_sem=meta_sem.at[0], recv_sem=meta_sem.at[1],
        device_id={"sub": other}, device_id_type=MESH,
    )
    meta_copy.start()

    def col_copy(d):
        idx, dev = col_peer(d)
        there = pl.ds(me_col * cl_dev, cl_dev)
        return pltpu.make_async_remote_copy(
            src_ref=col_half.at[dev["sub"]], dst_ref=col_buf.at[there],
            send_sem=col_ssem.at[d], recv_sem=col_rsem.at[d],
            device_id=dev, device_id_type=MESH,
        )

    def row_copy(d):
        idx, dev = row_peer(d)
        here = pl.ds(me_row * cl_dev, cl_dev)
        return pltpu.make_async_remote_copy(
            src_ref=row_buf.at[here], dst_ref=row_buf.at[here],
            send_sem=row_ssem.at[d], recv_sem=row_rsem.at[d],
            device_id=dev, device_id_type=MESH,
        )

    def col_arrived(d):
        idx = lax.rem(me_col + col_devs - d, col_devs)
        here = pl.ds(idx * cl_dev, cl_dev)
        pltpu.make_async_remote_copy(
            src_ref=col_half.at[0], dst_ref=col_buf.at[here],
            send_sem=col_ssem.at[d], recv_sem=col_rsem.at[d],
            device_id={"sub": other}, device_id_type=MESH,
        ).wait_recv()

    def row_arrived(d):
        idx = lax.rem(me_row + row_devs - d, row_devs)
        here = pl.ds(idx * cl_dev, cl_dev)
        pltpu.make_async_remote_copy(
            src_ref=row_buf.at[here], dst_ref=row_buf.at[here],
            send_sem=row_ssem.at[d], recv_sem=row_rsem.at[d],
            device_id={"sub": other}, device_id_type=MESH,
        ).wait_recv()

    for d in range(1, col_devs):
        col_copy(d).start()
    for d in range(1, row_devs):
        row_copy(d).start()

    meta_copy.wait()
    to_smem = pltpu.make_async_copy(meta, meta_s, local_sem)
    to_smem.start()
    to_smem.wait()
    for d in range(1, row_devs):
        row_arrived(d)
    for d in range(1, col_devs):
        col_arrived(d)

    first_rows = lax.broadcasted_iota(jnp.int32, (8, HALF), 0) < 4
    first_rows_wide = lax.broadcasted_iota(jnp.int32, (8, PANEL), 0) < 4

    def slot_of(k):
        count0 = jnp.where(s == 0, meta_s[0, 3, 0], meta_s[1, 3, 0])
        is_first = k < count0
        bank = jnp.where(is_first, s, 1 - s)
        at = jnp.where(is_first, k, k - count0)
        return meta_s[bank, 0, at], meta_s[bank, 1, at], meta_s[bank, 2, at]

    def swap(v):
        return jnp.concatenate([v[4:8], v[0:4]], axis=0)

    def one_slot(k, carry):
        v, u, q = slot_of(k)
        x_i = row_buf[v]
        y_j = col_buf[u]
        q_f = jnp.full((1, PANEL), q, jnp.int32).astype(F32)
        soften_sq = (SOFTEN / q_f) * (SOFTEN / q_f)
        t_j = jnp.transpose(y_j[0:8])
        for m in range(HALF // CHUNK):
            at = slice(m * CHUNK, (m + 1) * CHUNK)
            e = [x_i[a : a + 1] - t_j[at, a : a + 1] for a in range(3)]
            n_i = [x_i[3 + a : 4 + a] for a in range(3)]
            n_j = [t_j[at, 3 + a : 4 + a] for a in range(3)]
            for b, value in enumerate(tile_parts(e, n_i, n_j, soften_sq)):
                hi, lo = two_parts(value)
                tiles[b * 2 * HALF + m * CHUNK : b * 2 * HALF + (m + 1) * CHUNK, :] = hi
                tiles[b * 2 * HALF + HALF + m * CHUNK : b * 2 * HALF + HALF + (m + 1) * CHUNK, :] = lo
        d_j = y_j[8:16]
        s_j = swap(d_j)
        sig = jnp.where(first_rows, d_j, 0.0)
        mu = jnp.where(first_rows, s_j, 0.0)
        adj = jnp.where(first_rows, 0.0, -s_j)

        def stack_parts(value):
            hi = value.astype(BF16).astype(F32)
            return jnp.concatenate([hi, value - hi], axis=0).astype(BF16)

        sig, mu, adj = stack_parts(sig), stack_parts(mu), stack_parts(adj)
        lhs = jnp.concatenate([sig, sig, mu, mu, adj, adj], axis=1)
        got = jnp.dot(lhs, tiles[...], preferred_element_type=F32)
        row_term[k] = got[0:8] + got[8:16]
        lhs = stack_parts(x_i[8:16])
        got = lax.dot_general(lhs, tiles[...], (((1,), (1,)), ((), ())), preferred_element_type=F32)
        got = got[0:8] + got[8:16]
        t = [got[:, b * 2 * HALF : b * 2 * HALF + HALF] + got[:, b * 2 * HALF + HALF : (b + 1) * 2 * HALF] for b in range(3)]
        col_term[k] = jnp.where(first_rows, t[0] - swap(t[2]), swap(t[1]))
        return carry

    lax.fori_loop(0, used, one_slot, 0)

    slot_info = [slot_of(k) for k in range(used)]
    row_ids = [info[0] for info in slot_info]
    col_ids = []
    for v, u, _ in slot_info:
        a = r * (cl_dev * row_devs) + v
        per = n_sub * cl_dev
        b = ((u // per * n_col + c) * n_sub + lax.rem(u // cl_dev, n_sub)) * cl_dev + lax.rem(u, cl_dev)
        col_ids.append(jnp.where(a == b, -1, u))

    def col_sum(idx, g):
        total = jnp.zeros((8, HALF), F32)
        for k in range(used):
            total += jnp.where(col_ids[k] == idx * cl_dev + g, col_term[k], 0.0)
        return total

    def row_sum(idx, g):
        total = jnp.zeros((8, PANEL), F32)
        for k in range(used):
            total += jnp.where(row_ids[k] == idx * cl_dev + g, row_term[k], 0.0)
        return total

    def col_back(d):
        idx, dev = col_peer(d)
        return pltpu.make_async_remote_copy(
            src_ref=col_send.at[d], dst_ref=col_recv.at[me_col],
            send_sem=col_ssem2.at[d], recv_sem=col_rsem2.at[d],
            device_id=dev, device_id_type=MESH,
        )

    def row_back(d):
        idx, dev = row_peer(d)
        return pltpu.make_async_remote_copy(
            src_ref=row_send.at[d], dst_ref=row_recv.at[me_row],
            send_sem=row_ssem2.at[d], recv_sem=row_rsem2.at[d],
            device_id=dev, device_id_type=MESH,
        )

    def send_col(d, carry):
        for g in range(cl_dev):
            col_send[d, g] = col_sum(col_peer(d)[0], g)
        col_back(d).start()
        return carry

    def send_row(d, carry):
        for g in range(cl_dev):
            row_send[d, g] = row_sum(row_peer(d)[0], g)
        row_back(d).start()
        return carry

    lax.fori_loop(1, col_devs, send_col, 0)
    lax.fori_loop(1, row_devs, send_row, 0)
    for g in range(cl_dev):
        col_recv[me_col, g] = col_sum(me_col, g)
        row_recv[me_row, g] = row_sum(me_row, g)

    for d in range(1, row_devs):
        row_copy(d).wait_send()
    for d in range(1, col_devs):
        col_copy(d).wait_send()
    for d in range(1, row_devs):
        idx = lax.rem(me_row + row_devs - d, row_devs)
        pltpu.make_async_remote_copy(
            src_ref=row_send.at[d], dst_ref=row_recv.at[idx],
            send_sem=row_ssem2.at[d], recv_sem=row_rsem2.at[d],
            device_id={"sub": other}, device_id_type=MESH,
        ).wait_recv()
    for d in range(1, col_devs):
        idx = lax.rem(me_col + col_devs - d, col_devs)
        pltpu.make_async_remote_copy(
            src_ref=col_send.at[d], dst_ref=col_recv.at[idx],
            send_sem=col_ssem2.at[d], recv_sem=col_rsem2.at[d],
            device_id={"sub": other}, device_id_type=MESH,
        ).wait_recv()

    pieces = []
    for g in range(cl_dev):
        for h in range(2):
            total = row_recv[0, g, :, h * HALF : (h + 1) * HALF]
            for idx in range(1, row_devs):
                total += row_recv[idx, g, :, h * HALF : (h + 1) * HALF]
            for rr in range(n_row):
                total += col_recv[rr * n_sub + h, g]
            pieces.append(total)
    combined = jnp.concatenate(pieces, axis=1)
    parts = jnp.concatenate([three_parts(combined), jnp.zeros((8, own), F32)], axis=0).astype(BF16)
    for g in range(cl_dev):
        at = slice(g * PANEL, (g + 1) * PANEL)
        got = lax.dot_general(parts, onehot[at, :], (((1,), (1,)), ((), ())), preferred_element_type=F32)
        got = (got[0:8] + got[8:16]) + got[16:24]
        out_ref[0, :, at] = got[0:4] * wgt_ref[:, at]
        out_ref[1, :, at] = got[4:8]

    for d in range(1, row_devs):
        row_back(d).wait_send()
    for d in range(1, col_devs):
        col_back(d).wait_send()


def body(densities, positions, normals, weights, cluster_panels, pair_list, quad_order, pair_count):
    n_row, n_col, n_sub = (lax.axis_size(a) for a in ("row", "col", "sub"))
    own = positions.shape[1]
    cl_dev = own // PANEL
    slots = pair_list.shape[1]
    used = slots + slots // 4
    row_devs = n_col * n_sub
    col_devs = n_row * n_sub
    sizes = (n_row, n_col, n_sub, cl_dev, slots, used)
    dma = pltpu.SemaphoreType.DMA
    vmem = pltpu.VMEM
    return pl.pallas_call(
        functools.partial(kernel, sizes),
        out_shape=jax.ShapeDtypeStruct(densities.shape, F32),
        in_specs=[pl.BlockSpec(memory_space=pltpu.HBM)] * 8,
        out_specs=pl.BlockSpec(memory_space=pltpu.VMEM),
        scratch_shapes=[
            vmem(densities.shape, F32),
            vmem((3, own), F32),
            vmem((3, own), F32),
            vmem((1, own), F32),
            vmem((1, own), jnp.int32),
            vmem((2, slots), jnp.int32),
            vmem((1, slots), jnp.int32),
            vmem((1, 1), jnp.int32),
            dma((8,)),
            vmem((own, own), BF16),
            vmem((16, own), F32),
            vmem((2, 8, 128), jnp.int32),
            pltpu.SMEM((2, 8, 128), jnp.int32),
            vmem((row_devs * cl_dev, 16, PANEL), F32),
            vmem((2, cl_dev, 16, HALF), F32),
            vmem((col_devs * cl_dev, 16, HALF), F32),
            vmem((6 * HALF, PANEL), BF16),
            vmem((used, 8, PANEL), F32),
            vmem((used, 8, HALF), F32),
            vmem((row_devs, cl_dev, 8, PANEL), F32),
            vmem((col_devs, cl_dev, 8, HALF), F32),
            vmem((row_devs, cl_dev, 8, PANEL), F32),
            vmem((col_devs, cl_dev, 8, HALF), F32),
            dma((2,)),
            dma,
            dma((row_devs,)), dma((row_devs,)), dma((col_devs,)), dma((col_devs,)),
            dma((row_devs,)), dma((row_devs,)), dma((col_devs,)), dma((col_devs,)),
        ],
        compiler_params=pltpu.CompilerParams(
            collective_id=0, has_side_effects=True, vmem_limit_bytes=60 * 1024 * 1024
        ),
    )(
        densities, positions, normals, weights.reshape(1, own), cluster_panels,
        pair_list, quad_order.reshape(1, slots), pair_count.reshape(1, 1),
    )


def solution(mesh):
    split = ("groups", "row", "col", "sub")
    placed = (
        P(None, None, split), P(None, split), P(None, split), P(split),
        P(split, None), P(None, split), P(split), P(split),
    )
    return jax.shard_map(
        body, mesh=mesh, in_specs=placed, out_specs=P(None, None, split), check_vma=False
    )
```

```python
import functools
import math

import jax
import jax.numpy as jnp
import numpy as np
from jax import lax
from jax.experimental import pallas as pl
from jax.experimental.pallas import tpu as pltpu
from jax.sharding import PartitionSpec as P

MESH = pl.DeviceIdType.MESH
PANEL = 256
HALF = 128
WAVENUMBER = 3.0
SOFTEN = 0.5
FOUR_PI = 4.0 * math.pi
F32 = jnp.float32
BF16 = jnp.bfloat16
CHUNK = 16


def fit(func, degree):
    cheb = np.polynomial.chebyshev.Chebyshev.interpolate(func, degree, domain=[0.0, 0.2501])
    return [float(v) for v in cheb.convert(kind=np.polynomial.Polynomial).coef]


def sinc_turn(z):
    f = np.sqrt(np.maximum(z, 1e-30))
    return np.sin(2 * np.pi * f) / f


COS_COEF = [v / FOUR_PI for v in fit(lambda z: np.cos(2 * np.pi * np.sqrt(np.maximum(z, 0.0))), 5)]
SIN_COEF = [v * WAVENUMBER / FOUR_PI for v in fit(sinc_turn, 5)]


def horner(coef, z):
    value = coef[-1] * z + coef[-2]
    for c in coef[-3::-1]:
        value = value * z + c
    return value


def two_parts(value):
    hi = value.astype(BF16)
    lo = (value - hi.astype(F32)).astype(BF16)
    return hi, lo


def three_parts(value):
    hi = value.astype(BF16).astype(F32)
    rest = value - hi
    mid = rest.astype(BF16).astype(F32)
    return jnp.concatenate([hi, mid, rest - mid], axis=0)


def tile_parts(e, along_col, along_row, soften_sq):
    rho_sq = e[0] * e[0] + e[1] * e[1] + e[2] * e[2] + soften_sq
    inv = lax.rsqrt(rho_sq)
    rho = rho_sq * inv
    turns = rho * (WAVENUMBER / (2 * math.pi))
    f = turns - jnp.round(turns)
    z = f * f
    cosine = horner(COS_COEF, z)
    radial = (cosine + rho * f * horner(SIN_COEF, z)) * (inv * inv * inv)
    return cosine * inv, radial * along_col, radial * along_row


def kernel(
    sizes,
    dens_in, pos_in, nrm_in, wgt_in, order_in, pair_in, quad_in, count_in,
    out_ref,
    dens_ref, pos_ref, nrm_ref, wgt_ref, order_ref, pair_ref, quad_ref, count_ref, in_sem,
    onehot, stacked, meta, meta_s, row_buf, col_half, col_buf,
    tiles_a, tiles_b, tiles_c, row_term, col_term, row_send, col_send, row_recv, col_recv,
    meta_sem, local_sem, row_ssem, row_rsem, col_ssem, col_rsem,
    row_ssem2, row_rsem2, col_ssem2, col_rsem2,
):
    n_row, n_col, n_sub, cl_dev, slots, used = sizes
    own = cl_dev * PANEL
    tile_bufs = (tiles_a, tiles_b, tiles_c)
    row_devs = n_col * n_sub
    col_devs = n_row * n_sub
    r = lax.axis_index("row")
    c = lax.axis_index("col")
    s = lax.axis_index("sub")
    me_row = c * n_sub + s
    me_col = r * n_sub + s

    def row_peer(d):
        idx = lax.rem(me_row + d, row_devs)
        return idx, {"col": idx // n_sub, "sub": lax.rem(idx, n_sub)}

    def col_peer(d):
        idx = lax.rem(me_col + d, col_devs)
        return idx, {"row": idx // n_sub, "sub": lax.rem(idx, n_sub)}

    loads = [
        pltpu.make_async_copy(src, dst, in_sem.at[n])
        for n, (src, dst) in enumerate((
            (order_in, order_ref), (wgt_in, wgt_ref), (dens_in, dens_ref), (pos_in, pos_ref),
            (nrm_in, nrm_ref), (pair_in, pair_ref), (quad_in, quad_ref), (count_in, count_ref),
        ))
    ]
    for load in loads:
        load.start()
    barrier = pltpu.get_barrier_semaphore()
    for d in range(1, row_devs):
        pl.semaphore_signal(barrier, inc=1, device_id=row_peer(d)[1], device_id_type=MESH)
    for d in range(1, col_devs):
        pl.semaphore_signal(barrier, inc=1, device_id=col_peer(d)[1], device_id_type=MESH)

    loads[0].wait()
    def fill(t, carry):
        base = pl.multiple_of(t * 64, 64)
        ids = lax.broadcasted_iota(jnp.int32, (64, own), 0) + base
        onehot[pl.ds(base, 64), :] = jnp.where(ids == order_ref[...], 1.0, 0.0).astype(BF16)
        return carry

    lax.fori_loop(0, own // 64, fill, 0)

    for load in loads[1:]:
        load.wait()
    stacked[0:3, :] = pos_ref[...]
    stacked[3:6, :] = nrm_ref[...]
    stacked[6:8, :] = jnp.zeros((2, own), F32)
    stacked[8:12, :] = dens_ref[0] * wgt_ref[...]
    stacked[12:16, :] = dens_ref[1]
    meta[0] = jnp.zeros((8, 128), jnp.int32)
    meta[0, 0:2, 0:slots] = pair_ref[...]
    meta[0, 2:3, 0:slots] = quad_ref[...]
    meta[0, 3:4, 0:1] = count_ref[...]
    parts = three_parts(stacked[...]).astype(BF16)
    for g in range(cl_dev):
        got = jnp.dot(parts, onehot[:, g * PANEL : (g + 1) * PANEL], preferred_element_type=F32)
        panels = (got[0:16] + got[16:32]) + got[32:48]
        row_buf[me_row * cl_dev + g] = panels
        for h in range(2):
            col_half[h, g] = panels[:, h * HALF : (h + 1) * HALF]
    col_buf[pl.ds(me_col * cl_dev, cl_dev)] = col_half[s]

    pl.semaphore_wait(barrier, row_devs + col_devs - 2)

    other = 1 - s
    meta_copy = pltpu.make_async_remote_copy(
        src_ref=meta.at[0], dst_ref=meta.at[1], send_sem=meta_sem.at[0], recv_sem=meta_sem.at[1],
        device_id={"sub": other}, device_id_type=MESH,
    )
    meta_copy.start()

    def col_copy(d):
        idx, dev = col_peer(d)
        there = pl.ds(me_col * cl_dev, cl_dev)
        return pltpu.make_async_remote_copy(
            src_ref=col_half.at[dev["sub"]], dst_ref=col_buf.at[there],
            send_sem=col_ssem.at[d], recv_sem=col_rsem.at[d],
            device_id=dev, device_id_type=MESH,
        )

    def row_copy(d):
        idx, dev = row_peer(d)
        here = pl.ds(me_row * cl_dev, cl_dev)
        return pltpu.make_async_remote_copy(
            src_ref=row_buf.at[here], dst_ref=row_buf.at[here],
            send_sem=row_ssem.at[d], recv_sem=row_rsem.at[d],
            device_id=dev, device_id_type=MESH,
        )

    def col_arrived(d):
        idx = lax.rem(me_col + col_devs - d, col_devs)
        here = pl.ds(idx * cl_dev, cl_dev)
        pltpu.make_async_remote_copy(
            src_ref=col_half.at[0], dst_ref=col_buf.at[here],
            send_sem=col_ssem.at[d], recv_sem=col_rsem.at[d],
            device_id={"sub": other}, device_id_type=MESH,
        ).wait_recv()

    def row_arrived(d):
        idx = lax.rem(me_row + row_devs - d, row_devs)
        here = pl.ds(idx * cl_dev, cl_dev)
        pltpu.make_async_remote_copy(
            src_ref=row_buf.at[here], dst_ref=row_buf.at[here],
            send_sem=row_ssem.at[d], recv_sem=row_rsem.at[d],
            device_id={"sub": other}, device_id_type=MESH,
        ).wait_recv()

    for d in range(1, col_devs):
        col_copy(d).start()
    for d in range(1, row_devs):
        row_copy(d).start()

    meta_copy.wait()
    to_smem = pltpu.make_async_copy(meta, meta_s, local_sem)
    to_smem.start()
    to_smem.wait()
    for d in range(1, row_devs):
        row_arrived(d)
    for d in range(1, col_devs):
        col_arrived(d)

    first_rows = lax.broadcasted_iota(jnp.int32, (8, HALF), 0) < 4
    first_rows_wide = lax.broadcasted_iota(jnp.int32, (8, PANEL), 0) < 4

    def slot_of(k):
        count0 = jnp.where(s == 0, meta_s[0, 3, 0], meta_s[1, 3, 0])
        is_first = k < count0
        bank = jnp.where(is_first, s, 1 - s)
        at = jnp.where(is_first, k, k - count0)
        return meta_s[bank, 0, at], meta_s[bank, 1, at], meta_s[bank, 2, at]

    def swap(v):
        return jnp.concatenate([v[4:8], v[0:4]], axis=0)

    def split3(value):
        hi = value.astype(BF16).astype(F32)
        rest = value - hi
        mid = rest.astype(BF16).astype(F32)
        return hi, mid, rest - mid

    def left_parts(value):
        hi, mid, lo = split3(value)
        return jnp.concatenate([hi, hi, mid, hi, mid, lo], axis=0)

    def right_parts(value):
        hi, mid, lo = split3(value)
        return jnp.concatenate([hi, mid, hi, lo, mid, hi], axis=0)

    def dot3(a, b):
        return a[0:1] * b[0:1] + a[1:2] * b[1:2] + a[2:3] * b[2:3]

    def one_slot(k, tiles):
        v, u, q = slot_of(k)
        x_i = row_buf[v]
        y_j = col_buf[u]
        q_f = jnp.full((1, PANEL), q, jnp.int32).astype(F32)
        soften_sq = (SOFTEN / q_f) * (SOFTEN / q_f)
        x_in, n_in = x_i[0:3], x_i[3:6]
        x_jn, n_jn = y_j[0:3], y_j[3:6]
        pad_i, pad_j = jnp.zeros((4, PANEL), F32), jnp.zeros((4, HALF), F32)
        one_i, one_j = jnp.ones((1, PANEL), F32), jnp.ones((1, HALF), F32)
        to_col_l = left_parts(jnp.concatenate([n_jn, -dot3(x_jn, n_jn), pad_j], axis=0))
        to_row_l = left_parts(jnp.concatenate([-x_jn, one_j, pad_j], axis=0))
        to_col_r = right_parts(jnp.concatenate([x_in, one_i, pad_i], axis=0)).astype(BF16)
        to_row_r = right_parts(jnp.concatenate([n_in, dot3(x_in, n_in), pad_i], axis=0)).astype(BF16)
        t_j = jnp.transpose(y_j[0:8])
        along_col = jnp.dot(jnp.transpose(to_col_l).astype(BF16), to_col_r, preferred_element_type=F32)
        along_row = jnp.dot(jnp.transpose(to_row_l).astype(BF16), to_row_r, preferred_element_type=F32)
        for m in range(HALF // CHUNK):
            at = slice(m * CHUNK, (m + 1) * CHUNK)
            e = [x_i[a : a + 1] - t_j[at, a : a + 1] for a in range(3)]
            for b, value in enumerate(tile_parts(e, along_col[at], along_row[at], soften_sq)):
                hi, lo = two_parts(value)
                tiles[b * 2 * HALF + m * CHUNK : b * 2 * HALF + (m + 1) * CHUNK, :] = hi
                tiles[b * 2 * HALF + HALF + m * CHUNK : b * 2 * HALF + HALF + (m + 1) * CHUNK, :] = lo
        d_j = y_j[8:16]
        s_j = swap(d_j)
        sig = jnp.where(first_rows, d_j, 0.0)
        mu = jnp.where(first_rows, s_j, 0.0)
        adj = jnp.where(first_rows, 0.0, -s_j)

        def stack_parts(value):
            hi = value.astype(BF16).astype(F32)
            return jnp.concatenate([hi, value - hi], axis=0).astype(BF16)

        sig, mu, adj = stack_parts(sig), stack_parts(mu), stack_parts(adj)
        lhs = jnp.concatenate([sig, sig, mu, mu, adj, adj], axis=1)
        got = jnp.dot(lhs, tiles[...], preferred_element_type=F32)
        row_term[k] = got[0:8] + got[8:16]
        lhs = stack_parts(x_i[8:16])
        got = lax.dot_general(lhs, tiles[...], (((1,), (1,)), ((), ())), preferred_element_type=F32)
        got = got[0:8] + got[8:16]
        t = [got[:, b * 2 * HALF : b * 2 * HALF + HALF] + got[:, b * 2 * HALF + HALF : (b + 1) * 2 * HALF] for b in range(3)]
        col_term[k] = jnp.where(first_rows, t[0] - swap(t[2]), swap(t[1]))

    def some_slots(t, carry):
        for n, tiles in enumerate(tile_bufs):
            one_slot(t * len(tile_bufs) + n, tiles)
        return carry

    lax.fori_loop(0, used // len(tile_bufs), some_slots, 0)
    for n in range(used % len(tile_bufs)):
        one_slot(used - 1 - n, tile_bufs[n])

    slot_info = [slot_of(k) for k in range(used)]
    row_ids = [info[0] for info in slot_info]
    col_ids = []
    for v, u, _ in slot_info:
        a = r * (cl_dev * row_devs) + v
        per = n_sub * cl_dev
        b = ((u // per * n_col + c) * n_sub + lax.rem(u // cl_dev, n_sub)) * cl_dev + lax.rem(u, cl_dev)
        col_ids.append(jnp.where(a == b, -1, u))

    def col_sum(idx, g):
        total = jnp.zeros((8, HALF), F32)
        for k in range(used):
            total += jnp.where(col_ids[k] == idx * cl_dev + g, col_term[k], 0.0)
        return total

    def row_sum(idx, g):
        total = jnp.zeros((8, PANEL), F32)
        for k in range(used):
            total += jnp.where(row_ids[k] == idx * cl_dev + g, row_term[k], 0.0)
        return total

    def col_back(d):
        idx, dev = col_peer(d)
        return pltpu.make_async_remote_copy(
            src_ref=col_send.at[d], dst_ref=col_recv.at[me_col],
            send_sem=col_ssem2.at[d], recv_sem=col_rsem2.at[d],
            device_id=dev, device_id_type=MESH,
        )

    def row_back(d):
        idx, dev = row_peer(d)
        return pltpu.make_async_remote_copy(
            src_ref=row_send.at[d], dst_ref=row_recv.at[me_row],
            send_sem=row_ssem2.at[d], recv_sem=row_rsem2.at[d],
            device_id=dev, device_id_type=MESH,
        )

    def send_col(d, carry):
        for g in range(cl_dev):
            col_send[d, g] = col_sum(col_peer(d)[0], g)
        col_back(d).start()
        return carry

    def send_row(d, carry):
        for g in range(cl_dev):
            row_send[d, g] = row_sum(row_peer(d)[0], g)
        row_back(d).start()
        return carry

    lax.fori_loop(1, col_devs, send_col, 0)
    lax.fori_loop(1, row_devs, send_row, 0)
    for g in range(cl_dev):
        col_recv[me_col, g] = col_sum(me_col, g)
        row_recv[me_row, g] = row_sum(me_row, g)

    for d in range(1, row_devs):
        row_copy(d).wait_send()
    for d in range(1, col_devs):
        col_copy(d).wait_send()
    for d in range(1, row_devs):
        idx = lax.rem(me_row + row_devs - d, row_devs)
        pltpu.make_async_remote_copy(
            src_ref=row_send.at[d], dst_ref=row_recv.at[idx],
            send_sem=row_ssem2.at[d], recv_sem=row_rsem2.at[d],
            device_id={"sub": other}, device_id_type=MESH,
        ).wait_recv()
    for d in range(1, col_devs):
        idx = lax.rem(me_col + col_devs - d, col_devs)
        pltpu.make_async_remote_copy(
            src_ref=col_send.at[d], dst_ref=col_recv.at[idx],
            send_sem=col_ssem2.at[d], recv_sem=col_rsem2.at[d],
            device_id={"sub": other}, device_id_type=MESH,
        ).wait_recv()

    pieces = []
    for g in range(cl_dev):
        for h in range(2):
            total = row_recv[0, g, :, h * HALF : (h + 1) * HALF]
            for idx in range(1, row_devs):
                total += row_recv[idx, g, :, h * HALF : (h + 1) * HALF]
            for rr in range(n_row):
                total += col_recv[rr * n_sub + h, g]
            pieces.append(total)
    combined = jnp.concatenate(pieces, axis=1)
    parts = jnp.concatenate([three_parts(combined), jnp.zeros((8, own), F32)], axis=0).astype(BF16)
    for g in range(cl_dev):
        at = slice(g * PANEL, (g + 1) * PANEL)
        got = lax.dot_general(parts, onehot[at, :], (((1,), (1,)), ((), ())), preferred_element_type=F32)
        got = (got[0:8] + got[8:16]) + got[16:24]
        out_ref[0, :, at] = got[0:4] * wgt_ref[:, at]
        out_ref[1, :, at] = got[4:8]

    for d in range(1, row_devs):
        row_back(d).wait_send()
    for d in range(1, col_devs):
        col_back(d).wait_send()


def body(densities, positions, normals, weights, cluster_panels, pair_list, quad_order, pair_count):
    n_row, n_col, n_sub = (lax.axis_size(a) for a in ("row", "col", "sub"))
    own = positions.shape[1]
    cl_dev = own // PANEL
    slots = pair_list.shape[1]
    used = slots + slots // 4
    row_devs = n_col * n_sub
    col_devs = n_row * n_sub
    sizes = (n_row, n_col, n_sub, cl_dev, slots, used)
    dma = pltpu.SemaphoreType.DMA
    vmem = pltpu.VMEM
    return pl.pallas_call(
        functools.partial(kernel, sizes),
        out_shape=jax.ShapeDtypeStruct(densities.shape, F32),
        in_specs=[pl.BlockSpec(memory_space=pltpu.HBM)] * 8,
        out_specs=pl.BlockSpec(memory_space=pltpu.VMEM),
        scratch_shapes=[
            vmem(densities.shape, F32),
            vmem((3, own), F32),
            vmem((3, own), F32),
            vmem((1, own), F32),
            vmem((1, own), jnp.int32),
            vmem((2, slots), jnp.int32),
            vmem((1, slots), jnp.int32),
            vmem((1, 1), jnp.int32),
            dma((8,)),
            vmem((own, own), BF16),
            vmem((16, own), F32),
            vmem((2, 8, 128), jnp.int32),
            pltpu.SMEM((2, 8, 128), jnp.int32),
            vmem((row_devs * cl_dev, 16, PANEL), F32),
            vmem((2, cl_dev, 16, HALF), F32),
            vmem((col_devs * cl_dev, 16, HALF), F32),
            vmem((6 * HALF, PANEL), BF16),
            vmem((6 * HALF, PANEL), BF16),
            vmem((6 * HALF, PANEL), BF16),
            vmem((used, 8, PANEL), F32),
            vmem((used, 8, HALF), F32),
            vmem((row_devs, cl_dev, 8, PANEL), F32),
            vmem((col_devs, cl_dev, 8, HALF), F32),
            vmem((row_devs, cl_dev, 8, PANEL), F32),
            vmem((col_devs, cl_dev, 8, HALF), F32),
            dma((2,)),
            dma,
            dma((row_devs,)), dma((row_devs,)), dma((col_devs,)), dma((col_devs,)),
            dma((row_devs,)), dma((row_devs,)), dma((col_devs,)), dma((col_devs,)),
        ],
        compiler_params=pltpu.CompilerParams(
            collective_id=0, has_side_effects=True, vmem_limit_bytes=60 * 1024 * 1024
        ),
    )(
        densities, positions, normals, weights.reshape(1, own), cluster_panels,
        pair_list, quad_order.reshape(1, slots), pair_count.reshape(1, 1),
    )


def solution(mesh):
    split = ("groups", "row", "col", "sub")
    placed = (
        P(None, None, split), P(None, split), P(None, split), P(split),
        P(split, None), P(None, split), P(split), P(split),
    )
    return jax.shard_map(
        body, mesh=mesh, in_specs=placed, out_specs=P(None, None, split), check_vma=False
    )
```

```python
import functools
import math

import jax
import jax.numpy as jnp
import numpy as np
from jax import lax
from jax.experimental import pallas as pl
from jax.experimental.pallas import tpu as pltpu
from jax.sharding import PartitionSpec as P

MESH = pl.DeviceIdType.MESH
PANEL = 256
HALF = 128
WAVENUMBER = 3.0
SOFTEN = 0.5
FOUR_PI = 4.0 * math.pi
F32 = jnp.float32
BF16 = jnp.bfloat16
CHUNK = 16


def fit(func, degree):
    cheb = np.polynomial.chebyshev.Chebyshev.interpolate(func, degree, domain=[0.0, 0.2501])
    return [float(v) for v in cheb.convert(kind=np.polynomial.Polynomial).coef]


def sinc_turn(z):
    f = np.sqrt(np.maximum(z, 1e-30))
    return np.sin(2 * np.pi * f) / f


COS_COEF = [v / FOUR_PI for v in fit(lambda z: np.cos(2 * np.pi * np.sqrt(np.maximum(z, 0.0))), 5)]
SIN_COEF = [v * WAVENUMBER / FOUR_PI for v in fit(sinc_turn, 5)]


def horner(coef, z):
    value = coef[-1] * z + coef[-2]
    for c in coef[-3::-1]:
        value = value * z + c
    return value


def two_parts(value):
    hi = value.astype(BF16)
    lo = (value - hi.astype(F32)).astype(BF16)
    return hi, lo


def three_parts(value):
    hi = value.astype(BF16).astype(F32)
    rest = value - hi
    mid = rest.astype(BF16).astype(F32)
    return jnp.concatenate([hi, mid, rest - mid], axis=0)


def tile_parts(e, along_col, along_row, soften_sq):
    rho_sq = e[0] * e[0] + e[1] * e[1] + e[2] * e[2] + soften_sq
    inv = lax.rsqrt(rho_sq)
    rho = rho_sq * inv
    turns = rho * (WAVENUMBER / (2 * math.pi))
    f = turns - jnp.round(turns)
    z = f * f
    cosine = horner(COS_COEF, z)
    radial = (cosine + rho * f * horner(SIN_COEF, z)) * (inv * inv * inv)
    return cosine * inv, radial * along_col, radial * along_row


def kernel(
    sizes,
    dens_in, pos_in, nrm_in, wgt_in, order_in, pair_in, quad_in, count_in,
    out_ref,
    dens_ref, pos_ref, nrm_ref, wgt_ref, order_ref, pair_ref, quad_ref, count_ref, in_sem,
    onehot, stacked, meta, meta_s, row_geo, row_den, col_half, col_geo, col_den,
    tile_0, tile_1, tile_2, tile_3, tile_4, tile_5, tile_6, tile_7, tile_8, tile_9, row_term, col_term, row_send, col_send, row_recv, col_recv,
    meta_sem, local_sem, row_ssem, row_rsem, col_ssem, col_rsem,
    row_ssem2, row_rsem2, col_ssem2, col_rsem2,
):
    n_row, n_col, n_sub, cl_dev, slots, used = sizes
    own = cl_dev * PANEL
    row_buf = (row_geo, row_den)
    col_buf = (col_geo, col_den)
    tile_bufs = (tile_0, tile_1, tile_2, tile_3, tile_4, tile_5, tile_6, tile_7, tile_8, tile_9)
    row_devs = n_col * n_sub
    col_devs = n_row * n_sub
    r = lax.axis_index("row")
    c = lax.axis_index("col")
    s = lax.axis_index("sub")
    me_row = c * n_sub + s
    me_col = r * n_sub + s

    def row_peer(d):
        idx = lax.rem(me_row + d, row_devs)
        return idx, {"col": idx // n_sub, "sub": lax.rem(idx, n_sub)}

    def col_peer(d):
        idx = lax.rem(me_col + d, col_devs)
        return idx, {"row": idx // n_sub, "sub": lax.rem(idx, n_sub)}

    loads = [
        pltpu.make_async_copy(src, dst, in_sem.at[n])
        for n, (src, dst) in enumerate((
            (order_in, order_ref), (wgt_in, wgt_ref), (dens_in, dens_ref), (pos_in, pos_ref),
            (nrm_in, nrm_ref), (pair_in, pair_ref), (quad_in, quad_ref), (count_in, count_ref),
        ))
    ]
    for load in loads:
        load.start()
    barrier = pltpu.get_barrier_semaphore()
    for d in range(1, row_devs):
        pl.semaphore_signal(barrier, inc=1, device_id=row_peer(d)[1], device_id_type=MESH)
    for d in range(1, col_devs):
        pl.semaphore_signal(barrier, inc=1, device_id=col_peer(d)[1], device_id_type=MESH)

    loads[0].wait()
    def fill(t, carry):
        base = pl.multiple_of(t * 64, 64)
        ids = lax.broadcasted_iota(jnp.int32, (64, own), 0) + base
        onehot[pl.ds(base, 64), :] = jnp.where(ids == order_ref[...], 1.0, 0.0).astype(BF16)
        return carry

    lax.fori_loop(0, own // 64, fill, 0)

    for load in loads[1:]:
        load.wait()
    stacked[0:3, :] = pos_ref[...]
    stacked[3:6, :] = nrm_ref[...]
    stacked[6:8, :] = jnp.zeros((2, own), F32)
    stacked[8:12, :] = dens_ref[0] * wgt_ref[...]
    stacked[12:16, :] = dens_ref[1]
    meta[0] = jnp.zeros((8, 128), jnp.int32)
    meta[0, 0:2, 0:slots] = pair_ref[...]
    meta[0, 2:3, 0:slots] = quad_ref[...]
    meta[0, 3:4, 0:1] = count_ref[...]
    parts = three_parts(stacked[...]).astype(BF16)
    for g in range(cl_dev):
        got = jnp.dot(parts, onehot[:, g * PANEL : (g + 1) * PANEL], preferred_element_type=F32)
        panels = (got[0:16] + got[16:32]) + got[32:48]
        for kind in range(2):
            rows = panels[kind * 8 : (kind + 1) * 8]
            row_buf[kind][me_row * cl_dev + g] = rows
            for h in range(2):
                col_half[kind, h, g] = rows[:, h * HALF : (h + 1) * HALF]
    for kind in range(2):
        col_buf[kind][pl.ds(me_col * cl_dev, cl_dev)] = col_half[kind, s]

    pl.semaphore_wait(barrier, row_devs + col_devs - 2)

    other = 1 - s
    meta_copy = pltpu.make_async_remote_copy(
        src_ref=meta.at[0], dst_ref=meta.at[1], send_sem=meta_sem.at[0], recv_sem=meta_sem.at[1],
        device_id={"sub": other}, device_id_type=MESH,
    )
    meta_copy.start()

    def col_copy(kind, d):
        idx, dev = col_peer(d)
        there = pl.ds(me_col * cl_dev, cl_dev)
        return pltpu.make_async_remote_copy(
            src_ref=col_half.at[kind, dev["sub"]], dst_ref=col_buf[kind].at[there],
            send_sem=col_ssem.at[kind, d], recv_sem=col_rsem.at[kind, d],
            device_id=dev, device_id_type=MESH,
        )

    def row_copy(kind, d):
        idx, dev = row_peer(d)
        here = pl.ds(me_row * cl_dev, cl_dev)
        return pltpu.make_async_remote_copy(
            src_ref=row_buf[kind].at[here], dst_ref=row_buf[kind].at[here],
            send_sem=row_ssem.at[kind, d], recv_sem=row_rsem.at[kind, d],
            device_id=dev, device_id_type=MESH,
        )

    def col_arrived(kind, d):
        idx = lax.rem(me_col + col_devs - d, col_devs)
        here = pl.ds(idx * cl_dev, cl_dev)
        pltpu.make_async_remote_copy(
            src_ref=col_half.at[kind, 0], dst_ref=col_buf[kind].at[here],
            send_sem=col_ssem.at[kind, d], recv_sem=col_rsem.at[kind, d],
            device_id={"sub": other}, device_id_type=MESH,
        ).wait_recv()

    def row_arrived(kind, d):
        idx = lax.rem(me_row + row_devs - d, row_devs)
        here = pl.ds(idx * cl_dev, cl_dev)
        pltpu.make_async_remote_copy(
            src_ref=row_buf[kind].at[here], dst_ref=row_buf[kind].at[here],
            send_sem=row_ssem.at[kind, d], recv_sem=row_rsem.at[kind, d],
            device_id={"sub": other}, device_id_type=MESH,
        ).wait_recv()

    def all_arrived(kind):
        for d in range(1, row_devs):
            row_arrived(kind, d)
        for d in range(1, col_devs):
            col_arrived(kind, d)

    for kind in range(2):
        for d in range(1, col_devs):
            col_copy(kind, d).start()
        for d in range(1, row_devs):
            row_copy(kind, d).start()

    meta_copy.wait()
    to_smem = pltpu.make_async_copy(meta, meta_s, local_sem)
    to_smem.start()
    to_smem.wait()
    all_arrived(0)

    first_rows = lax.broadcasted_iota(jnp.int32, (8, HALF), 0) < 4
    first_rows_wide = lax.broadcasted_iota(jnp.int32, (8, PANEL), 0) < 4

    def slot_of(k):
        count0 = jnp.where(s == 0, meta_s[0, 3, 0], meta_s[1, 3, 0])
        is_first = k < count0
        bank = jnp.where(is_first, s, 1 - s)
        at = jnp.where(is_first, k, k - count0)
        return meta_s[bank, 0, at], meta_s[bank, 1, at], meta_s[bank, 2, at]

    def swap(v):
        return jnp.concatenate([v[4:8], v[0:4]], axis=0)

    def split3(value):
        hi = value.astype(BF16).astype(F32)
        rest = value - hi
        mid = rest.astype(BF16).astype(F32)
        return hi, mid, rest - mid

    def left_parts(value):
        hi, mid, lo = split3(value)
        return jnp.concatenate([hi, hi, mid, hi, mid, lo], axis=0)

    def right_parts(value):
        hi, mid, lo = split3(value)
        return jnp.concatenate([hi, mid, hi, lo, mid, hi], axis=0)

    def dot3(a, b):
        return a[0:1] * b[0:1] + a[1:2] * b[1:2] + a[2:3] * b[2:3]

    def make_tile(k, tiles):
        v, u, q = slot_of(k)
        x_i = row_geo[v]
        y_j = col_geo[u]
        q_f = jnp.full((1, PANEL), q, jnp.int32).astype(F32)
        soften_sq = (SOFTEN / q_f) * (SOFTEN / q_f)
        x_in, n_in = x_i[0:3], x_i[3:6]
        x_jn, n_jn = y_j[0:3], y_j[3:6]
        pad_i, pad_j = jnp.zeros((4, PANEL), F32), jnp.zeros((4, HALF), F32)
        one_i, one_j = jnp.ones((1, PANEL), F32), jnp.ones((1, HALF), F32)
        to_col_l = left_parts(jnp.concatenate([n_jn, -dot3(x_jn, n_jn), pad_j], axis=0))
        to_row_l = left_parts(jnp.concatenate([-x_jn, one_j, pad_j], axis=0))
        to_col_r = right_parts(jnp.concatenate([x_in, one_i, pad_i], axis=0)).astype(BF16)
        to_row_r = right_parts(jnp.concatenate([n_in, dot3(x_in, n_in), pad_i], axis=0)).astype(BF16)
        t_j = jnp.transpose(y_j)
        along_col = jnp.dot(jnp.transpose(to_col_l).astype(BF16), to_col_r, preferred_element_type=F32)
        along_row = jnp.dot(jnp.transpose(to_row_l).astype(BF16), to_row_r, preferred_element_type=F32)
        for m in range(HALF // CHUNK):
            at = slice(m * CHUNK, (m + 1) * CHUNK)
            e = [x_i[a : a + 1] - t_j[at, a : a + 1] for a in range(3)]
            for b, value in enumerate(tile_parts(e, along_col[at], along_row[at], soften_sq)):
                hi, lo = two_parts(value)
                tiles[b * 2 * HALF + m * CHUNK : b * 2 * HALF + (m + 1) * CHUNK, :] = hi
                tiles[b * 2 * HALF + HALF + m * CHUNK : b * 2 * HALF + HALF + (m + 1) * CHUNK, :] = lo

    def apply_tile(k, tiles):
        v, u, _ = slot_of(k)
        d_j = col_den[u]
        s_j = swap(d_j)
        sig = jnp.where(first_rows, d_j, 0.0)
        mu = jnp.where(first_rows, s_j, 0.0)
        adj = jnp.where(first_rows, 0.0, -s_j)

        def stack_parts(value):
            hi = value.astype(BF16).astype(F32)
            return jnp.concatenate([hi, value - hi], axis=0).astype(BF16)

        sig, mu, adj = stack_parts(sig), stack_parts(mu), stack_parts(adj)
        lhs = jnp.concatenate([sig, sig, mu, mu, adj, adj], axis=1)
        got = jnp.dot(lhs, tiles[...], preferred_element_type=F32)
        row_term[k] = got[0:8] + got[8:16]
        lhs = stack_parts(row_den[v])
        got = lax.dot_general(lhs, tiles[...], (((1,), (1,)), ((), ())), preferred_element_type=F32)
        got = got[0:8] + got[8:16]
        t = [got[:, b * 2 * HALF : b * 2 * HALF + HALF] + got[:, b * 2 * HALF + HALF : (b + 1) * 2 * HALF] for b in range(3)]
        col_term[k] = jnp.where(first_rows, t[0] - swap(t[2]), swap(t[1]))

    per_turn = 5
    turns = [range(t, min(t + per_turn, used)) for t in range(0, used, per_turn)]
    for n, turn in enumerate(turns):
        for k in turn:
            make_tile(k, tile_bufs[k % (2 * per_turn)])
            if n > 0 and k - per_turn in turns[n - 1]:
                apply_tile(k - per_turn, tile_bufs[(k - per_turn) % (2 * per_turn)])
        if n == 0:
            all_arrived(1)
    for k in range(used - per_turn, used):
        apply_tile(k, tile_bufs[k % (2 * per_turn)])

    slot_info = [slot_of(k) for k in range(used)]
    row_ids = [info[0] for info in slot_info]
    col_ids = []
    for v, u, _ in slot_info:
        a = r * (cl_dev * row_devs) + v
        per = n_sub * cl_dev
        b = ((u // per * n_col + c) * n_sub + lax.rem(u // cl_dev, n_sub)) * cl_dev + lax.rem(u, cl_dev)
        col_ids.append(jnp.where(a == b, -1, u))

    def col_sum(idx, g):
        total = jnp.zeros((8, HALF), F32)
        for k in range(used):
            total += jnp.where(col_ids[k] == idx * cl_dev + g, col_term[k], 0.0)
        return total

    def row_sum(idx, g):
        total = jnp.zeros((8, PANEL), F32)
        for k in range(used):
            total += jnp.where(row_ids[k] == idx * cl_dev + g, row_term[k], 0.0)
        return total

    def col_back(d):
        idx, dev = col_peer(d)
        return pltpu.make_async_remote_copy(
            src_ref=col_send.at[d], dst_ref=col_recv.at[me_col],
            send_sem=col_ssem2.at[d], recv_sem=col_rsem2.at[d],
            device_id=dev, device_id_type=MESH,
        )

    def row_back(d):
        idx, dev = row_peer(d)
        return pltpu.make_async_remote_copy(
            src_ref=row_send.at[d], dst_ref=row_recv.at[me_row],
            send_sem=row_ssem2.at[d], recv_sem=row_rsem2.at[d],
            device_id=dev, device_id_type=MESH,
        )

    def send_col(d, carry):
        for g in range(cl_dev):
            col_send[d, g] = col_sum(col_peer(d)[0], g)
        col_back(d).start()
        return carry

    def send_row(d, carry):
        for g in range(cl_dev):
            row_send[d, g] = row_sum(row_peer(d)[0], g)
        row_back(d).start()
        return carry

    lax.fori_loop(1, col_devs, send_col, 0)
    lax.fori_loop(1, row_devs, send_row, 0)
    for g in range(cl_dev):
        col_recv[me_col, g] = col_sum(me_col, g)
        row_recv[me_row, g] = row_sum(me_row, g)

    for d in range(1, row_devs):
        row_copy(0, d).wait_send()
        row_copy(1, d).wait_send()
    for d in range(1, col_devs):
        col_copy(0, d).wait_send()
        col_copy(1, d).wait_send()
    for d in range(1, row_devs):
        idx = lax.rem(me_row + row_devs - d, row_devs)
        pltpu.make_async_remote_copy(
            src_ref=row_send.at[d], dst_ref=row_recv.at[idx],
            send_sem=row_ssem2.at[d], recv_sem=row_rsem2.at[d],
            device_id={"sub": other}, device_id_type=MESH,
        ).wait_recv()
    for d in range(1, col_devs):
        idx = lax.rem(me_col + col_devs - d, col_devs)
        pltpu.make_async_remote_copy(
            src_ref=col_send.at[d], dst_ref=col_recv.at[idx],
            send_sem=col_ssem2.at[d], recv_sem=col_rsem2.at[d],
            device_id={"sub": other}, device_id_type=MESH,
        ).wait_recv()

    pieces = []
    for g in range(cl_dev):
        for h in range(2):
            total = row_recv[0, g, :, h * HALF : (h + 1) * HALF]
            for idx in range(1, row_devs):
                total += row_recv[idx, g, :, h * HALF : (h + 1) * HALF]
            for rr in range(n_row):
                total += col_recv[rr * n_sub + h, g]
            pieces.append(total)
    combined = jnp.concatenate(pieces, axis=1)
    parts = jnp.concatenate([three_parts(combined), jnp.zeros((8, own), F32)], axis=0).astype(BF16)
    for g in range(cl_dev):
        at = slice(g * PANEL, (g + 1) * PANEL)
        got = lax.dot_general(parts, onehot[at, :], (((1,), (1,)), ((), ())), preferred_element_type=F32)
        got = (got[0:8] + got[8:16]) + got[16:24]
        out_ref[0, :, at] = got[0:4] * wgt_ref[:, at]
        out_ref[1, :, at] = got[4:8]

    for d in range(1, row_devs):
        row_back(d).wait_send()
    for d in range(1, col_devs):
        col_back(d).wait_send()


def body(densities, positions, normals, weights, cluster_panels, pair_list, quad_order, pair_count):
    n_row, n_col, n_sub = (lax.axis_size(a) for a in ("row", "col", "sub"))
    own = positions.shape[1]
    cl_dev = own // PANEL
    slots = pair_list.shape[1]
    used = slots + slots // 4
    row_devs = n_col * n_sub
    col_devs = n_row * n_sub
    sizes = (n_row, n_col, n_sub, cl_dev, slots, used)
    dma = pltpu.SemaphoreType.DMA
    vmem = pltpu.VMEM
    return pl.pallas_call(
        functools.partial(kernel, sizes),
        out_shape=jax.ShapeDtypeStruct(densities.shape, F32),
        in_specs=[pl.BlockSpec(memory_space=pltpu.HBM)] * 8,
        out_specs=pl.BlockSpec(memory_space=pltpu.VMEM),
        scratch_shapes=[
            vmem(densities.shape, F32),
            vmem((3, own), F32),
            vmem((3, own), F32),
            vmem((1, own), F32),
            vmem((1, own), jnp.int32),
            vmem((2, slots), jnp.int32),
            vmem((1, slots), jnp.int32),
            vmem((1, 1), jnp.int32),
            dma((8,)),
            vmem((own, own), BF16),
            vmem((16, own), F32),
            vmem((2, 8, 128), jnp.int32),
            pltpu.SMEM((2, 8, 128), jnp.int32),
            *[vmem((row_devs * cl_dev, 8, PANEL), F32)] * 2,
            vmem((2, 2, cl_dev, 8, HALF), F32),
            *[vmem((col_devs * cl_dev, 8, HALF), F32)] * 2,
            *[vmem((6 * HALF, PANEL), BF16)] * 10,
            vmem((used, 8, PANEL), F32),
            vmem((used, 8, HALF), F32),
            vmem((row_devs, cl_dev, 8, PANEL), F32),
            vmem((col_devs, cl_dev, 8, HALF), F32),
            vmem((row_devs, cl_dev, 8, PANEL), F32),
            vmem((col_devs, cl_dev, 8, HALF), F32),
            dma((2,)),
            dma,
            dma((2, row_devs)), dma((2, row_devs)), dma((2, col_devs)), dma((2, col_devs)),
            dma((row_devs,)), dma((row_devs,)), dma((col_devs,)), dma((col_devs,)),
        ],
        compiler_params=pltpu.CompilerParams(
            collective_id=0, has_side_effects=True, vmem_limit_bytes=60 * 1024 * 1024
        ),
    )(
        densities, positions, normals, weights.reshape(1, own), cluster_panels,
        pair_list, quad_order.reshape(1, slots), pair_count.reshape(1, 1),
    )


def solution(mesh):
    split = ("groups", "row", "col", "sub")
    placed = (
        P(None, None, split), P(None, split), P(None, split), P(split),
        P(split, None), P(None, split), P(split), P(split),
    )
    return jax.shard_map(
        body, mesh=mesh, in_specs=placed, out_specs=P(None, None, split), check_vma=False
    )
```
